128 devices in a mesh: rows: 8 (over x_lo, z), lat: 16 (over y, x_hi, core).
Axes of the slice: x: 4 (x_hi: 2, x_lo: 2; x = x_hi * 2 + x_lo), y: 4, z: 4, core: 2. Of those that a mesh axis runs over, the one named last changes fastest.
Arguments:
- context: bfloat16 [768, 4096], P('rows', 'lat'), may hold values from -6 to 6
- out_weight: bfloat16 [4096, 4608], P('lat'), may hold values from -0.09375 to 0.09375
- residual: bfloat16 [768, 4608], P(('rows', 'lat')), may hold values from -6 to 6
- post_gain: float32 [4608], replicated, may hold values from 0.1 to 1.9
- enc_weight: bfloat16 [4608, 65536], P(None, ('rows', 'lat')), may hold values from -0.09375 to 0.09375
- enc_bias: float32 [65536], P(('rows', 'lat')), may hold values from -3 to 3
- thresholds: int32 [65536], P(('rows', 'lat')), may hold values from 2048 to 12287
- dec_weight: bfloat16 [65536, 4608], P(('rows', 'lat')), may hold values from -0.0234375 to 0.0234375
- dec_bias: float32 [4608], replicated, may hold values from -2 to 2
- first_moment: bfloat16 [65536, 4608], P(('rows', 'lat')), may hold values from -0.59765625 to 0.59765625
- second_moment: bfloat16 [65536, 4608], P(('rows', 'lat')), may hold values from 9.9658966e-05 to 0.0039978027
- pack_order: int32 [32], replicated, may hold values from 0 to 31, each once
- seq_lengths: int32 [8, 4], replicated, may hold values from 1 to 48, 96 in all within a row
Outputs:
- error: bfloat16 [768, 4608], P(('rows', 'lat'))
- adam_step: bfloat16 [65536, 4608], P(('rows', 'lat'))
The draws below stay inside these ranges and needn't reach their ends.
Inputs may be any that keep to these rules, and one draw needn't show every extreme that they name: `pack_order`: slot k lies in pack k // 4; every sequence number appears once. seq_lengths[p, j] belongs to slot p * 4 + j; the lengths of each pack sum to 96.
All inputs are finite; a program needn't handle non-finite values.
Results may differ from the reference program's by a relative error of at most 0.0082.
Values may be sent and summed in bfloat16 or wider, within the bound.
A program may use at most 128 MiB of HBM per device.

```python
import math
import jax
import jax.numpy as jnp
import numpy as np
from jax import lax

D = 4608
HEAD_DIM = 128
LATENTS = 65536
TOK_G = 96
SEQ_G = 4
HEADS = 32
TOKENS = 768
PACKS = 8
SEQS = 32


def plant(entries, key, low, largest):
    spot = [jax.random.randint(jax.random.fold_in(key, axis), (), 0, length) for axis, length in enumerate(entries.shape)]
    main_axis = entries.shape.index(max(entries.shape))
    next_to = spot[:main_axis] + [(spot[main_axis] + 1) % entries.shape[main_axis]] + spot[main_axis + 1:]
    return entries.at[tuple(spot)].set(low).at[tuple(next_to)].set(largest)


def block_levels(key, shape, split, least, top_value):
    level, own = 1.0, jax.random.fold_in(key, 6)
    for position, blocks in split:
        steps = jnp.exp(jax.random.uniform(jax.random.fold_in(own, position), (blocks,), jnp.float32, least / len(split), top_value / len(split)))
        level = level * jnp.repeat(steps, shape[position] // blocks).reshape([-1 if axis == position else 1 for axis in range(len(shape))])
    return level


def split_up(count, total, reach, slope):
    loads = [(1 << 20) // math.isqrt(grade ** slope) + 1 for grade in range(2, count + 1)]
    surplus, holding = total - reach - (count - 1), [1] * (count - 1)
    while surplus > 0:
        movable = [i for i in range(count - 1) if holding[i] < reach]
        whole, remaining = sum([loads[i] for i in movable]), surplus
        for i in movable:
            more = min(reach - holding[i], max(1, remaining * loads[i] // whole), surplus)
            holding[i] = holding[i] + more
            surplus = surplus - more
    return np.array([reach] + holding)


def ragged(own_key, count, total, limit, slope):
    if count == 2:
        one = jax.random.randint(own_key, (), max(1, total - limit), min(limit, total - 1) + 1)
        return jnp.stack([one, total - one])
    sizes = jnp.asarray(split_up(count, total, limit, slope), jnp.int32)
    twos = (count - 1) // 2
    giver, sink = sizes[1:1 + 2 * twos:2], sizes[2:2 + 2 * twos:2]
    slack = jnp.minimum(giver - 1, limit - sink)
    passed = jax.random.randint(jax.random.fold_in(own_key, 1), (twos,), 0, 1 << 20) % (slack + 1)
    sizes = sizes.at[1:1 + 2 * twos:2].set(giver - passed).at[2:2 + 2 * twos:2].set(sink + passed)
    return sizes[jax.random.permutation(jax.random.fold_in(own_key, 2), count)]


def normal_values(stream_key, dims, deviation, limit, split=(), kind=jnp.bfloat16):
    gain = block_levels(stream_key, dims, split, -0.22, 0.18) if split else 1.0
    result = jax.random.normal(stream_key, dims, jnp.float32) * deviation * gain
    return jnp.minimum(jnp.maximum(result, -limit), limit).astype(kind)


def setup_inputs(seed: int = 0) -> dict:
    key_of = jax.random.split(jax.random.key(seed), 14)
    return {
        "context": normal_values(key_of[0], (TOKENS, HEADS * HEAD_DIM), 1.0, 6.0, ((0, 8), (1, 16))),
        "out_weight": normal_values(key_of[1], (HEADS * HEAD_DIM, D), (HEADS * HEAD_DIM) ** -0.5, 0.09375, ((0, 16),)),
        "residual": normal_values(key_of[2], (TOKENS, D), 1.0, 6.0, ((0, 128),)),
        "post_gain": jnp.clip(1.0 + 0.18 * jax.random.normal(key_of[3], (D,), jnp.float32), 0.1, 1.9),
        "enc_weight": normal_values(key_of[4], (D, LATENTS), D ** -0.5, 0.09375, ((1, 128),)),
        "enc_bias": normal_values(key_of[5], (LATENTS,), 0.5, 3.0, ((0, 128),), jnp.float32),
        "thresholds": plant(jax.random.randint(key_of[6], (LATENTS,), 2048, 12288), jax.random.fold_in(key_of[6], 1), 2048, 12287).astype(jnp.int32),
        "dec_weight": normal_values(key_of[7], (LATENTS, D), LATENTS ** -0.5, 0.0234375, ((0, 128),)),
        "dec_bias": normal_values(key_of[8], (D,), 0.3, 2.0, (), jnp.float32),
        "first_moment": normal_values(key_of[9], (LATENTS, D), 0.1, 0.59765625, ((0, 128),)),
        "second_moment": jnp.clip(jnp.exp(math.log(0.0039978027) - 3.6917462 * jax.random.uniform(key_of[10], (LATENTS, D), jnp.float32) ** block_levels(key_of[10], (LATENTS, D), ((0, 128),), -0.2, 0.2)), 9.965896606445312e-05, 0.0039978027).astype(jnp.bfloat16),
        "pack_order": jax.random.permutation(key_of[11], SEQS).astype(jnp.int32),
        "seq_lengths": jax.vmap(lambda own: ragged(own, SEQ_G, TOK_G, TOK_G // 2, 2))(jax.random.split(key_of[12], PACKS)).reshape((PACKS, SEQ_G)).astype(jnp.int32),
    }


band_width = 0.25
beta_one = 0.9
beta_two = 0.999

def canonical_source(pack_order, seq_lengths, overall):
    lengths = seq_lengths.reshape(-1).astype(jnp.int32)
    slot_start = jnp.cumsum(lengths).astype(jnp.int32) - lengths
    seq_ids = jnp.arange(lengths.shape[0], dtype=jnp.int32)
    onehot = (pack_order[:, None] == seq_ids[None, :]).astype(jnp.int32)
    seq_length = lax.optimization_barrier(jnp.sum(onehot * lengths[:, None], axis=0)).astype(jnp.int32)
    seq_slot_start = lax.optimization_barrier(jnp.sum(onehot * slot_start[:, None], axis=0)).astype(jnp.int32)
    seq_start = jnp.cumsum(seq_length).astype(jnp.int32) - seq_length
    positions = jnp.arange(overall, dtype=jnp.int32)
    member = (positions[:, None] >= seq_start[None, :]).astype(jnp.int32)
    owner = lax.optimization_barrier(jnp.sum(member, axis=1)).astype(jnp.int32) - 1
    select = (owner[:, None] == seq_ids[None, :]).astype(jnp.int32)
    begin_canon = lax.optimization_barrier(jnp.sum(select * seq_start[None, :], axis=1)).astype(jnp.int32)
    begin_pack = lax.optimization_barrier(jnp.sum(select * seq_slot_start[None, :], axis=1)).astype(jnp.int32)
    return (begin_pack + positions - begin_canon).astype(jnp.int32)

def reference(context, out_weight, residual, post_gain, enc_weight, enc_bias, thresholds, dec_weight, dec_bias, first_moment, second_moment, pack_order, seq_lengths):
    attention = jnp.dot(context, out_weight, preferred_element_type=jnp.float32)
    root_mean = jnp.sqrt(lax.optimization_barrier(jnp.mean(attention * attention, axis=-1, keepdims=True)) + 1e-06)
    read = (residual.astype(jnp.float32) + post_gain * attention / root_mean).astype(jnp.bfloat16)
    source = canonical_source(pack_order, seq_lengths, TOKENS)
    canonical = jnp.take(read, source, axis=0)
    preact = jnp.dot(canonical, enc_weight, preferred_element_type=jnp.float32) + enc_bias
    cutoff = thresholds.astype(jnp.float32) / 4096.0
    active = (preact * jnp.clip((preact - cutoff) / band_width + 0.5, 0.0, 1.0)).astype(jnp.bfloat16)
    recon = jnp.dot(active, dec_weight, preferred_element_type=jnp.float32)
    error = (recon + dec_bias - canonical.astype(jnp.float32)).astype(jnp.bfloat16)
    blocks = 16
    block_rows = LATENTS // blocks
    active_blocks = active.T.reshape(blocks, block_rows, TOKENS)
    first_blocks = first_moment.reshape(blocks, block_rows, D)
    second_blocks = second_moment.reshape(blocks, block_rows, D)

    def adam_block(operands):
        act_block, first_block, second_block = operands
        gradient = jnp.dot(act_block, error, preferred_element_type=jnp.float32) / math.sqrt(TOKENS)
        moment_one = beta_one * first_block.astype(jnp.float32) + (1.0 - beta_one) * gradient
        moment_two = beta_two * second_block.astype(jnp.float32) + (1.0 - beta_two) * gradient * gradient
        update = moment_one / (1.0 - beta_one ** 2) / (jnp.sqrt(moment_two / (1.0 - beta_two ** 2)) + 1e-08)
        return update.astype(jnp.bfloat16)
    adam_step = lax.map(adam_block, (active_blocks, first_blocks, second_blocks)).reshape(LATENTS, D)
    return (error, adam_step)
```

```python
import math

import jax
import jax.numpy as jnp
from jax import lax
from jax.experimental import pallas as pl
from jax.experimental.pallas import tpu as pltpu
from jax.sharding import PartitionSpec as P

MESH = pl.DeviceIdType.MESH
F32 = jnp.float32
BF16 = jnp.bfloat16

D = 4608
TOKENS = 768
LOCAL = 512
QUART = 1152
SUB = 384
TILE = 16
THIRDS = range(3)
band_width = 0.25
beta_one = 0.9
beta_two = 0.999


def rem(a, b):
    return lax.rem(a, jnp.int32(b))


def tile_of(s, x, y, z):
    p = (x, y, z)
    i1, i2, i3 = p[s], p[(s + 1) % 3], p[(s + 2) % 3]
    return i1 // 2, i3, i2, i1 % 2


def columns_of(ref, t, y, s):
    return jnp.concatenate([ref[(s, t) + tile_of(s, x, y, z)] for x in range(4) for z in range(4)], axis=0)


def kernel(
    ctx, ow, res, gain, ebias, thr, dbias, porder, slens, enc_h, dec_h, m1_h, m2_h,
    err_o, adam_o,
    enc_v, dec_v, m1_v, m2_v, xb, pb, qb, eb, mb, fb, r2b, r1b,
    pa, sa, asum, sb, ar, rp, rr, stat, rb, act_t, gain_q, bias_q,
    load_sem, att_send, att_sib, att_recv, res_send, res_recv, stat_send, stat_recv,
    p1_send, p1_send0, p1_recv, ag_send, p2_recv, p3_recv, sib_recv,
    rs_send, q_recv, r3_recv, r2_recv, r1_recv, out_sem,
):
    r = lax.axis_index("rows")
    l = lax.axis_index("lat")
    c = rem(l, 2)
    xh = rem(l // 2, 2)
    y = l // 4
    xl = r // 4
    z = rem(r, 4)
    x = xh * 2 + xl
    own = c == xh
    me = (x, y, z)

    def device(x_, y_, z_, c_):
        return (rem(x_, 2) * 4 + z_, y_ * 4 + (x_ // 2) * 2 + c_)

    def ring(axis, d, core=None):
        p = [x, y, z]
        p[axis] = rem(p[axis] + d, 4)
        return device(*p, c if core is None else core)

    sibling = device(x, y, z, 1 - c)

    barrier = pltpu.get_barrier_semaphore()
    met = [(r, rem(l + d, 16)) for d in range(1, 16)]
    for core in range(2):
        met += [ring(0, 1, core), ring(0, 3, core)]
        met += [ring(2, d, core) for d in (1, 2, 3)]
    for dev in met:
        pl.semaphore_signal(barrier, inc=1, device_id=dev, device_id_type=MESH)

    loads = []
    for i, (h, v) in enumerate(((enc_h, enc_v), (dec_h, dec_v), (m1_h, m1_v), (m2_h, m2_v))):
        cp = pltpu.make_async_copy(h, v, load_sem.at[i])
        cp.start()
        loads.append(cp)

    for q in range(4):
        part = jnp.dot(ctx[...], ow[:, q * QUART:(q + 1) * QUART], preferred_element_type=F32)
        pa[q] = part.reshape(2, 48, QUART)
        sa[q] = pa[q, 1 - c].astype(BF16)
    rp[...] = jnp.zeros_like(rp)
    for q in range(4):
        cols = slice(q * QUART, (q + 1) * QUART)
        rp[q, 0:6] = res[:, cols]
        gain_q[q] = gain[cols].reshape(1, QUART)
        bias_q[q] = dbias[cols].reshape(1, QUART)

    def pick_rows():
        n = lax.broadcasted_iota(jnp.int32, (3, 256), 1)
        t = lax.broadcasted_iota(jnp.int32, (3, 256), 0)
        nx, nz, nr = n // 64, rem(n // 16, 4), rem(n, 16)
        token = (rem(nx, 2) * 4 + nz) * 96 + (nx // 2) * 48 + t * 16 + nr

        base = order = jnp.zeros((3, 256), jnp.int32)
        begin = jnp.int32(0)
        for k in range(32):
            end = begin + slens[k // 4, k % 4]
            inside = jnp.logical_and(token >= begin, token < end)
            base = jnp.where(inside, begin, base)
            order = jnp.where(inside, porder[k], order)
            begin = end
        place = token - base
        for k in range(32):
            place = place + jnp.where(porder[k] < order, slens[k // 4, k % 4], 0)
        first = (r * 16 + l) * 6
        for t in THIRDS:
            want = lax.broadcasted_iota(jnp.int32, (TILE, 256), 0) + first
            hit = jnp.logical_and(place[t:t + 1] == want, want < first + 6)
            act_t[t, LOCAL:LOCAL + TILE] = hit.astype(F32).astype(BF16)

    pick_rows()
    pl.semaphore_wait(barrier, len(met))

    def remote(src, dst, send, recv, dev):
        return pltpu.make_async_remote_copy(
            src_ref=src, dst_ref=dst, send_sem=send, recv_sem=recv, device_id=dev, device_id_type=MESH
        )

    def arrived(dst, sem):
        pltpu.make_async_copy(dst, dst, sem).wait()

    for d in (2, 1, 3, 0):
        q = rem(y + d, 4)
        remote(sa.at[q], asum.at[q], att_send.at[0], att_sib.at[q], sibling).start()
    rx = y // 2
    rslot = rem(y, 2) * 4 + xh * 2 + c
    stays = jnp.logical_and(rx == xh, c == rx)
    for d in (1, 2, 3):
        yd = rem(y + d, 4)
        remote(rp.at[yd], rr.at[rslot], res_send.at[0], res_recv.at[rslot], device(rx * 2 + xl, yd, z, rx)).start()

    @pl.when(stays)
    def _():
        pltpu.make_async_copy(rp.at[y], rr.at[rslot], res_recv.at[rslot]).start()

    @pl.when(jnp.logical_not(stays))
    def _():
        remote(rp.at[y], rr.at[rslot], res_send.at[1], res_recv.at[rslot], device(rx * 2 + xl, y, z, rx)).start()

    aslot = xh * 4 + y
    for d in (2, 1, 3, 0):
        yd = rem(y + d, 4)
        arrived(asum.at[yd], att_sib.at[yd])
        sb[yd] = (pa[yd, c] + asum[yd].astype(F32)).astype(BF16)
        if d:
            remote(sb.at[yd], ar.at[aslot], att_send.at[1], att_recv.at[aslot], device(c * 2 + xl, yd, z, c)).start()
        else:
            @pl.when(own)
            def _():
                pltpu.make_async_copy(sb.at[y], ar.at[aslot], att_recv.at[aslot]).start()

            @pl.when(jnp.logical_not(own))
            def _():
                remote(sb.at[y], ar.at[aslot], att_send.at[2], att_recv.at[aslot], device(c * 2 + xl, y, z, c)).start()

    def places(s):
        return me[s], me[(s + 1) % 3], me[(s + 2) % 3]

    def phase1(t):
        for s in THIRDS:
            i1, i2, i3 = places(s)
            k, j = i1 // 2, rem(i1, 2)
            src = rb.at[t, s]
            dst = xb.at[s, t, k, i3, i2, j]
            for d in (2, 1, 3):
                remote(src, dst, p1_send.at[0], p1_recv.at[t, s, j], ring(s, d, k)).start()

            @pl.when(k == c)
            def _():
                pltpu.make_async_copy(src, dst, p1_recv.at[t, s, j]).start()

            @pl.when(k != c)
            def _():
                remote(src, dst, p1_send0.at[s], p1_recv.at[t, s, j], sibling).start()

    def phase2(buf, w, t, s):
        i1, i2, i3 = places(s)
        piece = buf.at[s, t, c, i3, i2]
        for d in (2, 1, 3):
            remote(piece, piece, ag_send.at[w, 0], p2_recv.at[w, t, s, d], ring((s + 1) % 3, d)).start()

    def start_gather(t):
        for s in THIRDS:
            i1, i2, i3 = places(s)
            for j in range(2):
                arrived(xb.at[s, t, c, i3, i2, j], p1_recv.at[t, s, j])
            phase2(xb, 0, t, s)

    def phase3(buf, w, t):
        for s in THIRDS:
            i1, i2, i3 = places(s)
            for d in (1, 3, 2):
                arrived(buf.at[s, t, c, i3, rem(i2 + 4 - d, 4)], p2_recv.at[w, t, s, d])
            a3 = (s + 2) % 3
            half = [buf.at[s, t, c, i3, pl.ds(2 * h, 2)] for h in range(2)]
            for h in range(2):
                remote(half[h], half[h], ag_send.at[w, 1], p3_recv.at[w, t, s, 0, h], ring(a3, 1)).start()
                remote(half[1 - h], half[1 - h], ag_send.at[w, 1], p3_recv.at[w, t, s, 1, 1 - h], ring(a3, 3)).start()
        for s in THIRDS:
            share(buf, w, t, s, 0)

    def share(buf, w, t, s, d):
        part = buf.at[s, t, c, rem(places(s)[2] + d, 4)]
        remote(part, part, ag_send.at[w, 2], sib_recv.at[w, t, s, d], sibling).start()

    def forward(buf, w, t):
        for s in THIRDS:
            i3 = places(s)[2]
            a3 = (s + 2) % 3
            for side, d in ((0, 3), (1, 1)):
                piece = buf.at[s, t, c, rem(i3 + d, 4), pl.ds(2 * side, 2)]
                arrived(piece, p3_recv.at[w, t, s, side, side])
                remote(piece, piece, ag_send.at[w, 3], p3_recv.at[w, t, s, 2, side], ring(a3, 4 - d)).start()

    def finish_near(buf, w, t):
        for s in THIRDS:
            i3 = places(s)[2]
            for side, d in ((0, 3), (1, 1)):
                arrived(buf.at[s, t, c, rem(i3 + d, 4), pl.ds(2 - 2 * side, 2)], p3_recv.at[w, t, s, side, 1 - side])
                share(buf, w, t, s, d)

    def finish(buf, w, t):
        for s in THIRDS:
            i3 = places(s)[2]
            for side in range(2):
                arrived(buf.at[s, t, c, rem(i3 + 2, 4), pl.ds(2 * side, 2)], p3_recv.at[w, t, s, 2, side])
            share(buf, w, t, s, 2)

    def shared(buf, w, t):
        for s in THIRDS:
            i3 = places(s)[2]
            for d in range(4):
                arrived(buf.at[s, t, 1 - c, rem(i3 + d, 4)], sib_recv.at[w, t, s, d])

    def encode(t):
        rows = jnp.concatenate([columns_of(xb, t, q, s) for q in range(4) for s in THIRDS], axis=1)
        preact = jnp.dot(rows, enc_v[...], preferred_element_type=F32) + ebias[...]
        cutoff = thr[...].astype(F32) / 4096.0
        active = (preact * jnp.clip((preact - cutoff) / band_width + 0.5, 0.0, 1.0)).astype(BF16)
        act_t[t, 0:LOCAL] = active.T
        return active

    def decode(t, active):
        for q in range(4):
            part = jnp.dot(active, dec_v[:, q * QUART:(q + 1) * QUART], preferred_element_type=F32).astype(BF16)
            for s in THIRDS:
                for n in range(16):
                    pb[(s, t) + tile_of(s, n // 4, q, n % 4)] = part[n * TILE:(n + 1) * TILE, s * SUB:(s + 1) * SUB]
        for s in THIRDS:
            remote(pb.at[s, t, 1 - c], qb.at[s, t], rs_send.at[0], q_recv.at[t, s], sibling).start()

    def add_sibling(t, s, i3):
        return pb[s, t, c, i3].astype(F32) + qb[s, t, i3].astype(F32)

    def reduce_far(t):
        for s in THIRDS:
            i1, i2, i3 = places(s)
            a3 = (s + 2) % 3
            arrived(qb.at[s, t], q_recv.at[t, s])
            for d in (2, 1, 3):
                t3 = rem(i3 + d, 4)
                pb[s, t, c, t3] = add_sibling(t, s, t3).astype(BF16)
                for side in range(2):
                    src = pb.at[s, t, c, t3, pl.ds(2 * side, 2)]
                    if d == 2:
                        remote(src, mb.at[side, s, t], rs_send.at[1], r3_recv.at[t, s, 2, side], ring(a3, 1 + 2 * side)).start()
                    elif (d == 1) == (side == 1):
                        f = 0 if d == 1 else 1
                        remote(src, fb.at[f, s, t, pl.ds(2 * side, 2)], rs_send.at[2], r3_recv.at[t, s, f, side], ring(a3, d)).start()

    def reduce_near(t):
        for s in THIRDS:
            i1, i2, i3 = places(s)
            a3 = (s + 2) % 3
            for side, d in ((0, 1), (1, 3)):
                arrived(mb.at[side, s, t], r3_recv.at[t, s, 2, side])
                t3 = rem(i3 + d, 4)
                half = pl.ds(2 * side, 2)
                pb[s, t, c, t3, half] = (pb[s, t, c, t3, half].astype(F32) + mb[side, s, t].astype(F32)).astype(BF16)
                remote(pb.at[s, t, c, t3, half], fb.at[side, s, t, half], rs_send.at[2], r3_recv.at[t, s, side, side], ring(a3, d)).start()

    def reduce_mid(t):
        for s in THIRDS:
            i1, i2, i3 = places(s)
            total = add_sibling(t, s, i3)
            for f in range(2):
                for side in (1 - f, f):
                    arrived(fb.at[f, s, t, pl.ds(2 * side, 2)], r3_recv.at[t, s, f, side])
                total = total + fb[f, s, t].astype(F32)
            pb[s, t, c, i3] = total.astype(BF16)
            for d in (2, 1, 3):
                remote(pb.at[s, t, c, i3, rem(i2 + d, 4)], r2b.at[d - 1, s, t], rs_send.at[3], r2_recv.at[t, s, d],
                       ring((s + 1) % 3, d)).start()

    def reduce_last(t):
        for s in THIRDS:
            i1, i2, i3 = places(s)
            total = pb[s, t, c, i3, i2].astype(F32)
            for d in (1, 3, 2):
                arrived(r2b.at[d - 1, s, t], r2_recv.at[t, s, d])
                total = total + r2b[d - 1, s, t].astype(F32)
            r1b[s, t, i1] = total.astype(BF16)
            for d in (2, 1, 3):
                remote(r1b.at[s, t, i1], r1b.at[s, t, i1], rs_send.at[4], r1_recv.at[t, s, d], ring(s, d)).start()

    def make_error(t):
        for s in THIRDS:
            i1, i2, i3 = places(s)
            for d in (1, 3, 2):
                arrived(r1b.at[s, t, rem(i1 + 4 - d, 4)], r1_recv.at[t, s, d])
            for j in range(2):
                total = (r1b[s, t, 0, j].astype(F32) + r1b[s, t, 1, j].astype(F32)) + (
                    r1b[s, t, 2, j].astype(F32) + r1b[s, t, 3, j].astype(F32))
                bias = bias_q[2 * c + j if s == 1 else y, :, s * SUB:(s + 1) * SUB]
                canonical = xb[s, t, c, i3, i2, j].astype(F32)
                eb[s, t, c, i3, i2, j] = (total + bias - canonical).astype(BF16)
            phase2(eb, 1, t, s)

    @pl.when(own)
    def _():
        for i in range(8):
            arrived(ar.at[i], att_recv.at[i])
        att = ar[0].astype(F32)
        for i in range(1, 8):
            att = att + ar[i].astype(F32)
        stat[y] = jnp.broadcast_to(jnp.sum(att * att, axis=1, keepdims=True), (48, 128))
        for d in (2, 1, 3):
            remote(stat.at[y], stat.at[y], stat_send.at[0], stat_recv.at[y], ring(1, d)).start()
        for i in range(8):
            arrived(rr.at[i], res_recv.at[i])
        row = lax.broadcasted_iota(jnp.int32, (48, 128), 0)
        col = lax.broadcasted_iota(jnp.int32, (48, 128), 1)
        pick = (col == row + 10 * (row // 6)).astype(F32).astype(BF16)
        resid = jnp.dot(pick, rr[...].reshape(128, QUART), preferred_element_type=F32)
        scaled = gain_q[y] * att
        for d in (1, 3, 2):
            ys = rem(y + d, 4)
            arrived(stat.at[ys], stat_recv.at[ys])
        square = ((stat[0] + stat[1]) + (stat[2] + stat[3]))[:, 0:1]
        root_mean = jnp.sqrt(square / D + 1e-06)
        read = (resid + scaled / root_mean).astype(BF16)
        for t in THIRDS:
            for s in THIRDS:
                rb[t, s] = read[t * TILE:(t + 1) * TILE, s * SUB:(s + 1) * SUB]
            phase1(t)

    def update():
        loads[2].wait()
        loads[3].wait()
        one = 1.0 / (1.0 - beta_one**2)
        two = 1.0 / (1.0 - beta_two**2)
        copies = []
        for h in range(2):
            lo, hi = h * LOCAL // 2, (h + 1) * LOCAL // 2
            left = jnp.concatenate([act_t[t, lo:hi + h * TILE] for t in THIRDS], axis=1)
            for i in range(12):
                q, s = divmod(i, 3)
                cols = slice(q * QUART + s * SUB, q * QUART + (s + 1) * SUB)
                right = jnp.concatenate([columns_of(eb, t, q, s) for t in THIRDS], axis=0)
                grad = jnp.dot(left, right, preferred_element_type=F32)
                if h:
                    err_o[:, cols] = grad[hi - lo:hi - lo + 6].astype(BF16)
                g = grad[:hi - lo]
                first = (beta_one * one) * m1_v[lo:hi, cols].astype(F32) + ((1.0 - beta_one) * one / math.sqrt(TOKENS)) * g
                second = (beta_two * two) * m2_v[lo:hi, cols].astype(F32) + (((1.0 - beta_two) * two / TOKENS) * g) * g
                step = first * pltpu.reciprocal(second * lax.rsqrt(second) + 1e-08, approx=True)
                m1_v[lo:hi, cols] = step.astype(BF16)
            cp = pltpu.make_async_copy(m1_v.at[lo:hi], adam_o.at[lo:hi], out_sem.at[h])
            cp.start()
            copies.append(cp)
        for cp in copies:
            cp.wait()

    start_gather(0)
    start_gather(1)
    start_gather(2)
    phase3(xb, 0, 0)
    phase3(xb, 0, 1)
    forward(xb, 0, 0)
    phase3(xb, 0, 2)
    finish_near(xb, 0, 0)
    forward(xb, 0, 1)
    finish(xb, 0, 0)
    finish_near(xb, 0, 1)
    forward(xb, 0, 2)
    loads[0].wait()
    loads[1].wait()
    shared(xb, 0, 0)
    active = encode(0)
    finish(xb, 0, 1)
    finish_near(xb, 0, 2)
    decode(0, active)
    shared(xb, 0, 1)
    active = encode(1)
    finish(xb, 0, 2)
    reduce_far(0)
    decode(1, active)
    shared(xb, 0, 2)
    active = encode(2)
    reduce_near(0)
    reduce_far(1)
    decode(2, active)
    reduce_mid(0)
    reduce_near(1)
    reduce_far(2)
    reduce_last(0)
    reduce_mid(1)
    reduce_near(2)
    make_error(0)
    reduce_last(1)
    reduce_mid(2)
    phase3(eb, 1, 0)
    make_error(1)
    reduce_last(2)
    forward(eb, 1, 0)
    phase3(eb, 1, 1)
    make_error(2)
    finish_near(eb, 1, 0)
    forward(eb, 1, 1)
    phase3(eb, 1, 2)
    finish(eb, 1, 0)
    finish_near(eb, 1, 1)
    forward(eb, 1, 2)
    finish(eb, 1, 1)
    finish_near(eb, 1, 2)
    finish(eb, 1, 2)
    for t in THIRDS:
        shared(eb, 1, t)
    update()

    def sent(sem, n):
        for a in range(1, 4):
            for b in range(1, 4):
                for e in range(1, 5):
                    for f in range(1, 5):
                        if a * b * e * f * 2 == n:
                            view = xb.at[pl.ds(0, a), pl.ds(0, b), 0, pl.ds(0, e), pl.ds(0, f)]
                            pltpu.make_async_copy(view, view, sem).wait()
                            return
        if n % 64 == 0:
            view = xb.at[0, pl.ds(0, n // 64)]
        elif n % 9 == 0:
            view = xb.at[pl.ds(0, 3), pl.ds(0, 3), 0, pl.ds(0, n // 9), 0, 0]
        else:
            view = xb.at[0, pl.ds(0, n), 0, 0, 0, 0]
        assert math.prod(view.shape) == n * TILE * SUB
        pltpu.make_async_copy(view, view, sem).wait()

    sent(att_send.at[0], 36)
    sent(att_send.at[1], 27)
    sent(res_send.at[0], 9)

    @pl.when(jnp.logical_not(own))
    def _():
        sent(att_send.at[2], 9)

    @pl.when(jnp.logical_not(stays))
    def _():
        sent(res_send.at[1], 3)

    @pl.when(own)
    def _():
        pltpu.make_async_copy(stat.at[pl.ds(0, 3)], stat.at[pl.ds(0, 3)], stat_send.at[0]).wait()
        sent(p1_send.at[0], 27)
        for s in THIRDS:
            @pl.when(places(s)[0] // 2 != c)
            def _():
                sent(p1_send0.at[s], 3)

    for w in range(2):
        sent(ag_send.at[w, 0], 54)
        sent(ag_send.at[w, 1], 9 * 16)
        sent(ag_send.at[w, 2], 9 * 32)
        sent(ag_send.at[w, 3], 9 * 8)
    sent(rs_send.at[0], 9 * 32)
    sent(rs_send.at[1], 9 * 8)
    sent(rs_send.at[2], 9 * 16)
    sent(rs_send.at[3], 54)
    sent(rs_send.at[4], 54)


def body(context, out_weight, residual, post_gain, enc_weight, enc_bias, thresholds, dec_weight, dec_bias,
         first_moment, second_moment, pack_order, seq_lengths):
    vmem = pl.BlockSpec(memory_space=pltpu.VMEM)
    smem = pl.BlockSpec(memory_space=pltpu.SMEM)
    hbm = pl.BlockSpec(memory_space=pl.ANY)
    dma = pltpu.SemaphoreType.DMA

    def blocks(*dims):
        return pltpu.VMEM(dims + (TILE, SUB), BF16)

    scratch = [
        pltpu.VMEM((D, LOCAL), BF16), pltpu.VMEM((LOCAL, D), BF16),
        pltpu.VMEM((LOCAL, D), BF16), pltpu.VMEM((LOCAL, D), BF16),
        blocks(3, 3, 2, 4, 4, 2), blocks(3, 3, 2, 4, 4, 2), blocks(3, 3, 4, 4, 2), blocks(3, 3, 2, 4, 4, 2),
        blocks(2, 3, 3, 2, 2), blocks(2, 3, 3, 4, 2), blocks(3, 3, 3, 2), blocks(3, 3, 4, 2),
        pltpu.VMEM((4, 2, 48, QUART), F32), pltpu.VMEM((4, 48, QUART), BF16), pltpu.VMEM((4, 48, QUART), BF16),
        pltpu.VMEM((4, 48, QUART), BF16), pltpu.VMEM((8, 48, QUART), BF16),
        pltpu.VMEM((4, TILE, QUART), BF16), pltpu.VMEM((8, TILE, QUART), BF16),
        pltpu.VMEM((4, 48, 128), F32), blocks(3, 3),
        pltpu.VMEM((3, LOCAL + TILE, 16 * TILE), BF16),
        pltpu.VMEM((4, 1, QUART), F32), pltpu.VMEM((4, 1, QUART), F32),
        dma((4,)), dma((3,)), dma((4,)), dma((8,)), dma((2,)), dma((8,)), dma((1,)), dma((4,)),
        dma((1,)), dma((3,)), dma((3, 3, 2)), dma((2, 4)), dma((2, 3, 3, 4)), dma((2, 3, 3, 3, 2)), dma((2, 3, 3, 4)),
        dma((5,)), dma((3, 3)), dma((3, 3, 3, 2)), dma((3, 3, 4)), dma((3, 3, 4)), dma((12,)),
    ]
    return pl.pallas_call(
        kernel,
        out_shape=(jax.ShapeDtypeStruct((6, D), BF16), jax.ShapeDtypeStruct((LOCAL, D), BF16)),
        in_specs=[vmem] * 7 + [smem] * 2 + [hbm] * 4,
        out_specs=(vmem, hbm),
        scratch_shapes=scratch,
        compiler_params=pltpu.CompilerParams(
            collective_id=0, has_side_effects=True, vmem_limit_bytes=64 * 2**20
        ),
        cost_estimate=pl.CostEstimate(flops=11_100_000_000, bytes_accessed=31_000_000, transcendentals=0),
    )(
        context, out_weight, residual, post_gain, enc_bias.reshape(1, LOCAL),
        thresholds.reshape(1, LOCAL), dec_bias, pack_order, seq_lengths,
        enc_weight, dec_weight, first_moment, second_moment,
    )


def solution(mesh):
    return jax.shard_map(
        body,
        mesh=mesh,
        in_specs=(
            P("rows", "lat"), P("lat", None), P(("rows", "lat"), None), P(), P(None, ("rows", "lat")),
            P(("rows", "lat")), P(("rows", "lat")), P(("rows", "lat"), None), P(),
            P(("rows", "lat"), None), P(("rows", "lat"), None), P(), P(),
        ),
        out_specs=(P(("rows", "lat"), None), P(("rows", "lat"), None)),
        check_vma=False,
    )
```

```python
import math

import jax
import jax.numpy as jnp
from jax import lax
from jax.experimental import pallas as pl
from jax.experimental.pallas import tpu as pltpu
from jax.sharding import PartitionSpec as P

MESH = pl.DeviceIdType.MESH
F32 = jnp.float32
BF16 = jnp.bfloat16

D = 4608
TOKENS = 768
LOCAL = 512
QUART = 1152
SUB = 384
TILE = 16
THIRDS = range(3)
band_width = 0.25
beta_one = 0.9
beta_two = 0.999


def rem(a, b):
    return lax.rem(a, jnp.int32(b))


def tile_of(s, x, y, z):
    p = (x, y, z)
    i1, i2, i3 = p[s], p[(s + 1) % 3], p[(s + 2) % 3]
    return i1 // 2, i3, i2, i1 % 2


def columns_of(ref, t, y, s):
    return jnp.concatenate([ref[(s, t) + tile_of(s, x, y, z)] for x in range(4) for z in range(4)], axis=0)


def kernel(
    ctx, ow, res, gain, ebias, thr, dbias, porder, slens, enc_h, dec_h, m1_h, m2_h,
    err_o, adam_o,
    enc_v, dec_v, m1_v, m2_v, xb, pb, qb, eb, mb, fb, r2b, r1b,
    pa, sa, asum, sb, ar, rp, rr, stat, rb, att_v, res_v, act_t, gain_q, bias_q,
    load_sem, att_send, att_sib, att_recv, res_send, res_recv, stat_send, stat_recv,
    p1_send, p1_send0, p1_recv, ag_send, p2_recv, p3_recv, sib_recv,
    rs_send, q_recv, r3_recv, r2_recv, r1_recv, out_sem,
):
    r = lax.axis_index("rows")
    l = lax.axis_index("lat")
    c = rem(l, 2)
    xh = rem(l // 2, 2)
    y = l // 4
    xl = r // 4
    z = rem(r, 4)
    x = xh * 2 + xl
    own = c == xh
    me = (x, y, z)

    def device(x_, y_, z_, c_):
        return (rem(x_, 2) * 4 + z_, y_ * 4 + (x_ // 2) * 2 + c_)

    def ring(axis, d, core=None):
        p = [x, y, z]
        p[axis] = rem(p[axis] + d, 4)
        return device(*p, c if core is None else core)

    sibling = device(x, y, z, 1 - c)

    barrier = pltpu.get_barrier_semaphore()
    met = [(r, rem(l + d, 16)) for d in range(1, 16)]
    for core in range(2):
        met += [ring(0, 1, core), ring(0, 3, core)]
        met += [ring(2, d, core) for d in (1, 2, 3)]
    for dev in met:
        pl.semaphore_signal(barrier, inc=1, device_id=dev, device_id_type=MESH)

    for q in range(4):
        part = jnp.dot(ctx[...], ow[:, q * QUART:(q + 1) * QUART], preferred_element_type=F32)
        pa[q] = part.reshape(2, 48, QUART)
        sa[q] = pa[q, 1 - c].astype(BF16)
    rp[...] = jnp.zeros_like(rp)
    for q in range(4):
        cols = slice(q * QUART, (q + 1) * QUART)
        rp[q, 0:6] = res[:, cols]
        gain_q[q] = gain[cols].reshape(1, QUART)
        bias_q[q] = dbias[cols].reshape(1, QUART)

    def pick_rows():
        n = lax.broadcasted_iota(jnp.int32, (3, 256), 1)
        t = lax.broadcasted_iota(jnp.int32, (3, 256), 0)
        nx, nz, nr = n // 64, rem(n // 16, 4), rem(n, 16)
        token = (rem(nx, 2) * 4 + nz) * 96 + (nx // 2) * 48 + t * 16 + nr

        base = order = jnp.zeros((3, 256), jnp.int32)
        begin = jnp.int32(0)
        for k in range(32):
            end = begin + slens[k // 4, k % 4]
            inside = jnp.logical_and(token >= begin, token < end)
            base = jnp.where(inside, begin, base)
            order = jnp.where(inside, porder[k], order)
            begin = end
        place = token - base
        for k in range(32):
            place = place + jnp.where(porder[k] < order, slens[k // 4, k % 4], 0)
        first = (r * 16 + l) * 6
        for t in THIRDS:
            want = lax.broadcasted_iota(jnp.int32, (TILE, 256), 0) + first
            hit = jnp.logical_and(place[t:t + 1] == want, want < first + 6)
            act_t[t, LOCAL:LOCAL + TILE] = hit.astype(F32).astype(BF16)

    pl.semaphore_wait(barrier, len(met))

    def remote(src, dst, send, recv, dev):
        return pltpu.make_async_remote_copy(
            src_ref=src, dst_ref=dst, send_sem=send, recv_sem=recv, device_id=dev, device_id_type=MESH
        )

    def arrived(dst, sem):
        pltpu.make_async_copy(dst, dst, sem).wait()

    for d in (2, 1, 3, 0):
        q = rem(y + d, 4)
        remote(sa.at[q], asum.at[q], att_send.at[0], att_sib.at[q], sibling).start()
    aslot = xh * 4 + y

    def exchange(t):
        rows = slice(t * TILE, (t + 1) * TILE)
        for d in (2, 1, 3, 0):
            yd = rem(y + d, 4)
            if t == 0:
                arrived(asum.at[yd], att_sib.at[yd])
            sb[t, yd] = (pa[yd, c, rows] + asum[yd, rows].astype(F32)).astype(BF16)
            dst = ar.at[t, aslot]
            if d:
                remote(sb.at[t, yd], dst, att_send.at[1], att_recv.at[t, aslot], device(c * 2 + xl, yd, z, c)).start()
            else:
                @pl.when(own)
                def _():
                    pltpu.make_async_copy(sb.at[t, y], dst, att_recv.at[t, aslot]).start()

                @pl.when(jnp.logical_not(own))
                def _():
                    remote(sb.at[t, y], dst, att_send.at[2], att_recv.at[t, aslot], device(c * 2 + xl, y, z, c)).start()

    exchange(0)
    rx = y // 2
    rslot = rem(y, 2) * 4 + xh * 2 + c
    stays = jnp.logical_and(rx == xh, c == rx)
    for d in (1, 2, 3):
        yd = rem(y + d, 4)
        remote(rp.at[yd], rr.at[rslot], res_send.at[0], res_recv.at[rslot], device(rx * 2 + xl, yd, z, rx)).start()

    @pl.when(stays)
    def _():
        pltpu.make_async_copy(rp.at[y], rr.at[rslot], res_recv.at[rslot]).start()

    @pl.when(jnp.logical_not(stays))
    def _():
        remote(rp.at[y], rr.at[rslot], res_send.at[1], res_recv.at[rslot], device(rx * 2 + xl, y, z, rx)).start()

    exchange(1)
    exchange(2)

    def places(s):
        return me[s], me[(s + 1) % 3], me[(s + 2) % 3]

    def phase1(t):
        for s in THIRDS:
            i1, i2, i3 = places(s)
            k, j = i1 // 2, rem(i1, 2)
            src = rb.at[t, s]
            dst = xb.at[s, t, k, i3, i2, j]
            for d in (2, 1, 3):
                remote(src, dst, p1_send.at[0], p1_recv.at[t, s, j], ring(s, d, k)).start()

            @pl.when(k == c)
            def _():
                pltpu.make_async_copy(src, dst, p1_recv.at[t, s, j]).start()

            @pl.when(k != c)
            def _():
                remote(src, dst, p1_send0.at[s], p1_recv.at[t, s, j], sibling).start()

    def phase2(buf, w, t, s):
        i1, i2, i3 = places(s)
        piece = buf.at[s, t, c, i3, i2]
        for d in (2, 1, 3):
            remote(piece, piece, ag_send.at[w, 0], p2_recv.at[w, t, s, d], ring((s + 1) % 3, d)).start()

    def start_gather(t):
        for s in THIRDS:
            i1, i2, i3 = places(s)
            for j in range(2):
                arrived(xb.at[s, t, c, i3, i2, j], p1_recv.at[t, s, j])
            phase2(xb, 0, t, s)

    def phase3(buf, w, t):
        for s in THIRDS:
            i1, i2, i3 = places(s)
            for d in (1, 3, 2):
                arrived(buf.at[s, t, c, i3, rem(i2 + 4 - d, 4)], p2_recv.at[w, t, s, d])
            a3 = (s + 2) % 3
            half = [buf.at[s, t, c, i3, pl.ds(2 * h, 2)] for h in range(2)]
            for h in range(2):
                remote(half[h], half[h], ag_send.at[w, 1], p3_recv.at[w, t, s, 0, h], ring(a3, 1)).start()
                remote(half[1 - h], half[1 - h], ag_send.at[w, 1], p3_recv.at[w, t, s, 1, 1 - h], ring(a3, 3)).start()
        for s in THIRDS:
            share(buf, w, t, s, 0)

    def share(buf, w, t, s, d):
        part = buf.at[s, t, c, rem(places(s)[2] + d, 4)]
        remote(part, part, ag_send.at[w, 2], sib_recv.at[w, t, s, d], sibling).start()

    def forward(buf, w, t):
        for s in THIRDS:
            i3 = places(s)[2]
            a3 = (s + 2) % 3
            for side, d in ((0, 3), (1, 1)):
                piece = buf.at[s, t, c, rem(i3 + d, 4), pl.ds(2 * side, 2)]
                arrived(piece, p3_recv.at[w, t, s, side, side])
                remote(piece, piece, ag_send.at[w, 3], p3_recv.at[w, t, s, 2, side], ring(a3, 4 - d)).start()

    def finish_near(buf, w, t):
        for s in THIRDS:
            i3 = places(s)[2]
            for side, d in ((0, 3), (1, 1)):
                arrived(buf.at[s, t, c, rem(i3 + d, 4), pl.ds(2 - 2 * side, 2)], p3_recv.at[w, t, s, side, 1 - side])
                share(buf, w, t, s, d)

    def finish(buf, w, t):
        for s in THIRDS:
            i3 = places(s)[2]
            for side in range(2):
                arrived(buf.at[s, t, c, rem(i3 + 2, 4), pl.ds(2 * side, 2)], p3_recv.at[w, t, s, 2, side])
            share(buf, w, t, s, 2)

    def shared(buf, w, t):
        for s in THIRDS:
            i3 = places(s)[2]
            for d in range(4):
                arrived(buf.at[s, t, 1 - c, rem(i3 + d, 4)], sib_recv.at[w, t, s, d])

    def encode(t):
        rows = jnp.concatenate([columns_of(xb, t, q, s) for q in range(4) for s in THIRDS], axis=1)
        preact = jnp.dot(rows, enc_v[...], preferred_element_type=F32) + ebias[...]
        cutoff = thr[...].astype(F32) / 4096.0
        active = (preact * jnp.clip((preact - cutoff) / band_width + 0.5, 0.0, 1.0)).astype(BF16)
        act_t[t, 0:LOCAL] = active.T
        return active

    def decode(t, active):
        for q in range(4):
            part = jnp.dot(active, dec_v[:, q * QUART:(q + 1) * QUART], preferred_element_type=F32).astype(BF16)
            for s in THIRDS:
                for n in range(16):
                    pb[(s, t) + tile_of(s, n // 4, q, n % 4)] = part[n * TILE:(n + 1) * TILE, s * SUB:(s + 1) * SUB]
        for s in THIRDS:
            remote(pb.at[s, t, 1 - c], qb.at[s, t], rs_send.at[0], q_recv.at[t, s], sibling).start()

    def add_sibling(t, s, i3):
        return pb[s, t, c, i3].astype(F32) + qb[s, t, i3].astype(F32)

    def reduce_far(t):
        for s in THIRDS:
            i1, i2, i3 = places(s)
            a3 = (s + 2) % 3
            arrived(qb.at[s, t], q_recv.at[t, s])
            for d in (2, 1, 3):
                t3 = rem(i3 + d, 4)
                pb[s, t, c, t3] = add_sibling(t, s, t3).astype(BF16)
                for side in range(2):
                    src = pb.at[s, t, c, t3, pl.ds(2 * side, 2)]
                    if d == 2:
                        remote(src, mb.at[side, s, t], rs_send.at[1], r3_recv.at[t, s, 2, side], ring(a3, 1 + 2 * side)).start()
                    elif (d == 1) == (side == 1):
                        f = 0 if d == 1 else 1
                        remote(src, fb.at[f, s, t, pl.ds(2 * side, 2)], rs_send.at[2], r3_recv.at[t, s, f, side], ring(a3, d)).start()

    def reduce_near(t):
        for s in THIRDS:
            i1, i2, i3 = places(s)
            a3 = (s + 2) % 3
            for side, d in ((0, 1), (1, 3)):
                arrived(mb.at[side, s, t], r3_recv.at[t, s, 2, side])
                t3 = rem(i3 + d, 4)
                half = pl.ds(2 * side, 2)
                pb[s, t, c, t3, half] = (pb[s, t, c, t3, half].astype(F32) + mb[side, s, t].astype(F32)).astype(BF16)
                remote(pb.at[s, t, c, t3, half], fb.at[side, s, t, half], rs_send.at[2], r3_recv.at[t, s, side, side], ring(a3, d)).start()

    def reduce_mid(t):
        for s in THIRDS:
            i1, i2, i3 = places(s)
            total = add_sibling(t, s, i3)
            for f in range(2):
                for side in (1 - f, f):
                    arrived(fb.at[f, s, t, pl.ds(2 * side, 2)], r3_recv.at[t, s, f, side])
                total = total + fb[f, s, t].astype(F32)
            pb[s, t, c, i3] = total.astype(BF16)
            for d in (2, 1, 3):
                remote(pb.at[s, t, c, i3, rem(i2 + d, 4)], r2b.at[d - 1, s, t], rs_send.at[3], r2_recv.at[t, s, d],
                       ring((s + 1) % 3, d)).start()

    def reduce_last(t):
        for s in THIRDS:
            i1, i2, i3 = places(s)
            total = pb[s, t, c, i3, i2].astype(F32)
            for d in (1, 3, 2):
                arrived(r2b.at[d - 1, s, t], r2_recv.at[t, s, d])
                total = total + r2b[d - 1, s, t].astype(F32)
            r1b[s, t, i1] = total.astype(BF16)
            for d in (2, 1, 3):
                remote(r1b.at[s, t, i1], r1b.at[s, t, i1], rs_send.at[4], r1_recv.at[t, s, d], ring(s, d)).start()

    def make_error(t):
        for s in THIRDS:
            i1, i2, i3 = places(s)
            for d in (1, 3, 2):
                arrived(r1b.at[s, t, rem(i1 + 4 - d, 4)], r1_recv.at[t, s, d])
            for j in range(2):
                total = (r1b[s, t, 0, j].astype(F32) + r1b[s, t, 1, j].astype(F32)) + (
                    r1b[s, t, 2, j].astype(F32) + r1b[s, t, 3, j].astype(F32))
                bias = bias_q[2 * c + j if s == 1 else y, :, s * SUB:(s + 1) * SUB]
                canonical = xb[s, t, c, i3, i2, j].astype(F32)
                eb[s, t, c, i3, i2, j] = (total + bias - canonical).astype(BF16)
            phase2(eb, 1, t, s)

    def add_up(t):
        for i in range(8):
            arrived(ar.at[t, i], att_recv.at[t, i])
        att = ar[t, 0].astype(F32)
        for i in range(1, 8):
            att = att + ar[t, i].astype(F32)
        att_v[t] = att
        stat[t, y] = jnp.broadcast_to(jnp.sum(att * att, axis=1, keepdims=True), (TILE, 128))
        for d in (2, 1, 3):
            remote(stat.at[t, y], stat.at[t, y], stat_send.at[0], stat_recv.at[t, y], ring(1, d)).start()

    def place_residual():
        for i in range(8):
            arrived(rr.at[i], res_recv.at[i])
        row = lax.broadcasted_iota(jnp.int32, (48, 128), 0)
        col = lax.broadcasted_iota(jnp.int32, (48, 128), 1)
        pick = (col == row + 10 * (row // 6)).astype(F32).astype(BF16)
        resid = jnp.dot(pick, rr[...].reshape(128, QUART), preferred_element_type=F32)
        res_v[...] = resid.reshape(3, TILE, QUART)

    def normalise(t):
        for d in (1, 3, 2):
            ys = rem(y + d, 4)
            arrived(stat.at[t, ys], stat_recv.at[t, ys])
        square = ((stat[t, 0] + stat[t, 1]) + (stat[t, 2] + stat[t, 3]))[:, 0:1]
        root_mean = jnp.sqrt(square / D + 1e-06)
        read = (res_v[t] + gain_q[y] * att_v[t] / root_mean).astype(BF16)
        for s in THIRDS:
            rb[t, s] = read[:, s * SUB:(s + 1) * SUB]
        phase1(t)

    @pl.when(own)
    def _():
        add_up(0)
        place_residual()
        add_up(1)
        normalise(0)
        add_up(2)
        normalise(1)

    def update():
        loads[2].wait()
        loads[3].wait()
        one = 1.0 / (1.0 - beta_one**2)
        two = 1.0 / (1.0 - beta_two**2)
        copies = []
        for h in range(2):
            lo, hi = h * LOCAL // 2, (h + 1) * LOCAL // 2
            left = jnp.concatenate([act_t[t, lo:hi + h * TILE] for t in THIRDS], axis=1)
            for i in range(12):
                q, s = divmod(i, 3)
                cols = slice(q * QUART + s * SUB, q * QUART + (s + 1) * SUB)
                right = jnp.concatenate([columns_of(eb, t, q, s) for t in THIRDS], axis=0)
                grad = jnp.dot(left, right, preferred_element_type=F32)
                if h:
                    err_o[:, cols] = grad[hi - lo:hi - lo + 6].astype(BF16)
                g = grad[:hi - lo]
                first = (beta_one * one) * m1_v[lo:hi, cols].astype(F32) + ((1.0 - beta_one) * one / math.sqrt(TOKENS)) * g
                second = (beta_two * two) * m2_v[lo:hi, cols].astype(F32) + (((1.0 - beta_two) * two / TOKENS) * g) * g
                step = first * pltpu.reciprocal(second * lax.rsqrt(second) + 1e-08, approx=True)
                m1_v[lo:hi, cols] = step.astype(BF16)
            cp = pltpu.make_async_copy(m1_v.at[lo:hi], adam_o.at[lo:hi], out_sem.at[h])
            cp.start()
            copies.append(cp)
        for cp in copies:
            cp.wait()

    def load(i, src, dst):
        cp = pltpu.make_async_copy(src, dst, load_sem.at[i])
        cp.start()
        return cp

    loads = [load(0, enc_h, enc_v), load(1, dec_h, dec_v)]
    start_gather(0)

    @pl.when(own)
    def _():
        normalise(2)

    start_gather(1)
    phase3(xb, 0, 0)
    start_gather(2)
    phase3(xb, 0, 1)
    pick_rows()
    loads += [load(2, m1_h, m1_v), load(3, m2_h, m2_v)]
    forward(xb, 0, 0)
    phase3(xb, 0, 2)
    finish_near(xb, 0, 0)
    forward(xb, 0, 1)
    finish_near(xb, 0, 1)
    finish(xb, 0, 0)
    loads[0].wait()
    loads[1].wait()
    shared(xb, 0, 0)
    active = encode(0)
    forward(xb, 0, 2)
    decode(0, active)
    finish(xb, 0, 1)
    finish_near(xb, 0, 2)
    shared(xb, 0, 1)
    active = encode(1)
    finish(xb, 0, 2)
    reduce_far(0)
    decode(1, active)
    shared(xb, 0, 2)
    active = encode(2)
    reduce_far(1)
    reduce_near(0)
    decode(2, active)
    reduce_near(1)
    reduce_far(2)
    reduce_mid(0)
    reduce_near(2)
    reduce_mid(1)
    reduce_last(0)
    reduce_mid(2)
    reduce_last(1)
    make_error(0)
    reduce_last(2)
    make_error(1)
    make_error(2)
    phase3(eb, 1, 0)
    phase3(eb, 1, 1)
    phase3(eb, 1, 2)
    forward(eb, 1, 0)
    forward(eb, 1, 1)
    forward(eb, 1, 2)
    finish_near(eb, 1, 0)
    finish_near(eb, 1, 1)
    finish_near(eb, 1, 2)
    finish(eb, 1, 0)
    finish(eb, 1, 1)
    finish(eb, 1, 2)
    for t in THIRDS:
        shared(eb, 1, t)
    update()

    def sent(sem, n):
        for a in range(1, 4):
            for b in range(1, 4):
                for e in range(1, 5):
                    for f in range(1, 5):
                        if a * b * e * f * 2 == n:
                            view = xb.at[pl.ds(0, a), pl.ds(0, b), 0, pl.ds(0, e), pl.ds(0, f)]
                            pltpu.make_async_copy(view, view, sem).wait()
                            return
        if n % 64 == 0:
            view = xb.at[0, pl.ds(0, n // 64)]
        elif n % 9 == 0:
            view = xb.at[pl.ds(0, 3), pl.ds(0, 3), 0, pl.ds(0, n // 9), 0, 0]
        else:
            view = xb.at[0, pl.ds(0, n), 0, 0, 0, 0]
        assert math.prod(view.shape) == n * TILE * SUB
        pltpu.make_async_copy(view, view, sem).wait()

    sent(att_send.at[0], 36)
    sent(att_send.at[1], 27)
    sent(res_send.at[0], 9)

    @pl.when(jnp.logical_not(own))
    def _():
        sent(att_send.at[2], 9)

    @pl.when(jnp.logical_not(stays))
    def _():
        sent(res_send.at[1], 3)

    @pl.when(own)
    def _():
        pltpu.make_async_copy(stat.at[pl.ds(0, 3), pl.ds(0, 3)], stat.at[pl.ds(0, 3), pl.ds(0, 3)], stat_send.at[0]).wait()
        sent(p1_send.at[0], 27)
        for s in THIRDS:
            @pl.when(places(s)[0] // 2 != c)
            def _():
                sent(p1_send0.at[s], 3)

    for w in range(2):
        sent(ag_send.at[w, 0], 54)
        sent(ag_send.at[w, 1], 9 * 16)
        sent(ag_send.at[w, 2], 9 * 32)
        sent(ag_send.at[w, 3], 9 * 8)
    sent(rs_send.at[0], 9 * 32)
    sent(rs_send.at[1], 9 * 8)
    sent(rs_send.at[2], 9 * 16)
    sent(rs_send.at[3], 54)
    sent(rs_send.at[4], 54)


def body(context, out_weight, residual, post_gain, enc_weight, enc_bias, thresholds, dec_weight, dec_bias,
         first_moment, second_moment, pack_order, seq_lengths):
    vmem = pl.BlockSpec(memory_space=pltpu.VMEM)
    smem = pl.BlockSpec(memory_space=pltpu.SMEM)
    hbm = pl.BlockSpec(memory_space=pl.ANY)
    dma = pltpu.SemaphoreType.DMA

    def blocks(*dims):
        return pltpu.VMEM(dims + (TILE, SUB), BF16)

    scratch = [
        pltpu.VMEM((D, LOCAL), BF16), pltpu.VMEM((LOCAL, D), BF16),
        pltpu.VMEM((LOCAL, D), BF16), pltpu.VMEM((LOCAL, D), BF16),
        blocks(3, 3, 2, 4, 4, 2), blocks(3, 3, 2, 4, 4, 2), blocks(3, 3, 4, 4, 2), blocks(3, 3, 2, 4, 4, 2),
        blocks(2, 3, 3, 2, 2), blocks(2, 3, 3, 4, 2), blocks(3, 3, 3, 2), blocks(3, 3, 4, 2),
        pltpu.VMEM((4, 2, 48, QUART), F32), pltpu.VMEM((4, 48, QUART), BF16), pltpu.VMEM((4, 48, QUART), BF16),
        pltpu.VMEM((3, 4, TILE, QUART), BF16), pltpu.VMEM((3, 8, TILE, QUART), BF16),
        pltpu.VMEM((4, TILE, QUART), BF16), pltpu.VMEM((8, TILE, QUART), BF16),
        pltpu.VMEM((3, 4, TILE, 128), F32), blocks(3, 3), pltpu.VMEM((3, TILE, QUART), F32), pltpu.VMEM((3, TILE, QUART), F32),
        pltpu.VMEM((3, LOCAL + TILE, 16 * TILE), BF16),
        pltpu.VMEM((4, 1, QUART), F32), pltpu.VMEM((4, 1, QUART), F32),
        dma((4,)), dma((3,)), dma((4,)), dma((3, 8)), dma((2,)), dma((8,)), dma((1,)), dma((3, 4)),
        dma((1,)), dma((3,)), dma((3, 3, 2)), dma((2, 4)), dma((2, 3, 3, 4)), dma((2, 3, 3, 3, 2)), dma((2, 3, 3, 4)),
        dma((5,)), dma((3, 3)), dma((3, 3, 3, 2)), dma((3, 3, 4)), dma((3, 3, 4)), dma((12,)),
    ]
    return pl.pallas_call(
        kernel,
        out_shape=(jax.ShapeDtypeStruct((6, D), BF16), jax.ShapeDtypeStruct((LOCAL, D), BF16)),
        in_specs=[vmem] * 7 + [smem] * 2 + [hbm] * 4,
        out_specs=(vmem, hbm),
        scratch_shapes=scratch,
        compiler_params=pltpu.CompilerParams(
            collective_id=0, has_side_effects=True, vmem_limit_bytes=64 * 2**20
        ),
        cost_estimate=pl.CostEstimate(flops=11_100_000_000, bytes_accessed=31_000_000, transcendentals=0),
    )(
        context, out_weight, residual, post_gain, enc_bias.reshape(1, LOCAL),
        thresholds.reshape(1, LOCAL), dec_bias, pack_order, seq_lengths,
        enc_weight, dec_weight, first_moment, second_moment,
    )


def solution(mesh):
    return jax.shard_map(
        body,
        mesh=mesh,
        in_specs=(
            P("rows", "lat"), P("lat", None), P(("rows", "lat"), None), P(), P(None, ("rows", "lat")),
            P(("rows", "lat")), P(("rows", "lat")), P(("rows", "lat"), None), P(),
            P(("rows", "lat"), None), P(("rows", "lat"), None), P(), P(),
        ),
        out_specs=(P(("rows", "lat"), None), P(("rows", "lat"), None)),
        check_vma=False,
    )
```
